32 devices in a mesh: owner: 4 (over x, core), shard: 8 (over z, y).
Axes of the slice: x: 2, y: 2, z: 4, core: 2. Of those that a mesh axis runs over, the one named last changes fastest.
Arguments:
- tokens: bfloat16 [96, 7168], P('shard', 'owner'), may hold values from -6 to 6
- expert_ids: int32 [96, 8], P('shard'), may hold values from 0 to 47, all different within a row; in each aligned block of 12 rows (0 to 11, 12 to 23, ...) at most 3 rows name the same one
- gate_weight: bfloat16 [48, 7168, 1024], P('shard', 'owner'), may hold values from -0.0625 to 0.0625
- up_weight: bfloat16 [48, 7168, 1024], P('shard', 'owner'), may hold values from -0.0625 to 0.0625
- trainer_down: float32 [48, 1024, 7168], P('shard', None, 'owner'), may hold values from -0.1875 to 0.1875
Outputs:
- hidden: bfloat16 [24, 48, 1024], P('owner', 'shard')
- new_down: bfloat16 [48, 1024, 7168], P('shard', 'owner')
The draws below stay inside these ranges and needn't reach their ends.
Inputs may be any that keep to these rules, and one draw needn't show every extreme that they name: `expert_ids`: within the rows of one index of shard (aligned blocks of 12 rows) no expert is named by more than 3 rows, a bound that some block reaches.
All inputs are finite; a program needn't handle non-finite values.
Results may differ from the reference program's by a relative error of at most 0.0017.
Values may be sent and summed in bfloat16 or wider, within the bound.
A program may use at most 256 MiB of HBM per device.

```python
import math
import jax
import jax.numpy as jnp
import numpy as np
from jax import lax

D = 7168
TOP = 8
FF = 1024
EXPERTS = 48
ROWS_DEV = 12
CAP = 3
ROWS = 96
N_SHARD = 8


def shard_levels(stream_key, shape, pieces, least, top_value):
    def one(position, parts):
        steps = jax.random.uniform(jax.random.fold_in(jax.random.fold_in(stream_key, 6), position), (parts,), jnp.float32, least / len(pieces), top_value / len(pieces))
        return jnp.repeat(jnp.exp(steps), shape[position] // parts).reshape((-1,) + (1,) * (len(shape) - position - 1))

    factor_of = one(*pieces[0])
    for cut in pieces[1:]:
        factor_of = factor_of * one(*cut)
    return factor_of


def routed_block(own_key, own, number, rows, number_of, top, reach, slope):
    ranking = jax.random.permutation(own_key, number_of)
    heavy_load, ordinary = load_shares(number_of, rows * top, reach, slope, True), load_shares(number_of, rows * top, reach, slope, False)
    places = jnp.arange(number_of)

    def named(tallies, rotation):
        used = int((tallies > 0).sum())
        fixed = max(1, used // 4)
        moved = fixed + (places - fixed + rotation * (used - fixed)) % max(1, number_of - fixed)
        return jnp.zeros((number_of,), jnp.int32).at[ranking[jnp.where(places < fixed, places, moved)]].set(jnp.asarray(tallies, jnp.int32))

    tallies = jnp.where(number % 4 == 0, named(heavy_load, number // 4), named(ordinary, number - number // 4 - 1))
    mixed = jax.random.permutation(jax.random.fold_in(own, 3), number_of)
    donor, taker = mixed[0:number_of // 2 * 2:2], mixed[1:number_of // 2 * 2:2]
    slack = jnp.minimum(tallies[donor] - 1, reach - tallies[taker]) // 2
    slack = jnp.where((donor == ranking[0]) | (taker == ranking[0]) | (tallies[taker] == 0), 0, jnp.maximum(slack, 0))
    moved = jax.random.randint(jax.random.fold_in(own, 4), (number_of // 2,), 0, 1 << 20) % (slack + 1)
    tallies = tallies.at[donor].add(-moved).at[taker].add(moved)
    labels = jnp.searchsorted(jnp.cumsum(tallies), jnp.arange(rows * top), side="right").astype(jnp.int32)
    grid = labels.reshape(top, rows).T
    grid = grid[jax.random.permutation(jax.random.fold_in(own, 1), rows)]
    rotation = jax.random.randint(jax.random.fold_in(own, 2), (rows, 1), 0, top)
    return jnp.take_along_axis(grid, (jnp.arange(top)[None, :] + rotation) % top, axis=1)


def load_shares(count, total, reach, slope, full):
    loads = [(1 << 20) // math.isqrt(rank ** slope) + 1 for rank in range(1, count + 1)]
    largest = reach if full else min(reach, max(-(-total // count), total * loads[0] // sum(loads)))
    least = 1 if total - largest >= count - 1 else 0
    given, spare = [largest] + [least] * (count - 1), total - largest - least * (count - 1)
    while spare > 0:
        free = [i for i in range(1, count) if given[i] < largest] or [i for i in range(1, count) if given[i] < reach]
        mass, remaining = sum([loads[i] for i in free]), spare
        for i in free:
            addition = min(reach - given[i], max(1, remaining * loads[i] // mass), spare)
            given[i] = given[i] + addition
            spare = spare - addition
    return np.array(given)


def centred(stream_key, extent, spread, reach, pieces=(), kind=jnp.bfloat16):
    entries = spread * jax.random.normal(stream_key, extent, jnp.float32)
    if pieces:
        entries = entries * shard_levels(stream_key, extent, pieces, -0.22, 0.18)
    return jnp.clip(entries, -reach, reach).astype(kind)


def setup_inputs(seed: int = 0) -> dict:
    arg_keys = jax.random.split(jax.random.key(seed), 6)
    tokens = centred(arg_keys[0], (ROWS, D), 1.0, 6.0, ((0, 8), (1, 4)))
    expert_ids_keys = jax.random.split(jax.random.fold_in(arg_keys[1], 1), ROWS // ROWS_DEV)
    expert_ids_turns = jax.random.permutation(jax.random.fold_in(arg_keys[1], 3), ROWS // ROWS_DEV)
    expert_ids = jax.vmap(lambda own, number: routed_block(jax.random.fold_in(arg_keys[1], 2), own, number, ROWS_DEV, EXPERTS, TOP, CAP, 2))(expert_ids_keys, expert_ids_turns).reshape((ROWS, TOP))
    gate_weight = centred(arg_keys[2], (EXPERTS, D, FF), D ** -0.5, 0.0625, ((0, 8), (1, 4)))
    up_weight = centred(arg_keys[3], (EXPERTS, D, FF), D ** -0.5, 0.0625, ((0, 8), (1, 4)))
    trainer_down = centred(arg_keys[4], (EXPERTS, FF, D), FF ** -0.5, 0.1875, ((0, 8), (2, 4)), jnp.float32)
    return dict(tokens=tokens, expert_ids=expert_ids, gate_weight=gate_weight, up_weight=up_weight, trainer_down=trainer_down)


def place_block(block):
    block_tokens, block_ids = block
    flat = block_ids.reshape(-1)
    hits = (flat[:, None] == jnp.arange(EXPERTS, dtype=jnp.int32)[None, :]).astype(jnp.int32)
    before = jnp.cumsum(hits, axis=0) - hits
    place = jnp.sum(before * hits, axis=1)
    target = place * EXPERTS + flat
    select = (target[:, None] == jnp.arange(CAP * EXPERTS, dtype=jnp.int32)[None, :]).astype(jnp.int32)
    select = jnp.sum(select.reshape(ROWS_DEV, TOP, CAP * EXPERTS), axis=1).astype(block_tokens.dtype)
    sent = jnp.dot(select.T, block_tokens, preferred_element_type=jnp.float32)
    return sent.astype(jnp.bfloat16).reshape(CAP, EXPERTS, D)


def reference(tokens, expert_ids, gate_weight, up_weight, trainer_down):
    token_blocks = tokens.reshape(N_SHARD, ROWS_DEV, D)
    id_blocks = expert_ids.reshape(N_SHARD, ROWS_DEV, TOP)
    sends = lax.map(place_block, (token_blocks, id_blocks))
    dispatched = sends.reshape(N_SHARD * CAP, EXPERTS, D)
    by_expert = jnp.swapaxes(dispatched, 0, 1)

    def one_expert(item):
        rows, gate_one, up_one = item
        gate = jnp.dot(rows, gate_one, preferred_element_type=jnp.float32)
        up = jnp.dot(rows, up_one, preferred_element_type=jnp.float32)
        return (jax.nn.silu(gate) * up).astype(jnp.bfloat16)

    hidden = lax.map(one_expert, (by_expert, gate_weight, up_weight))
    hidden = jnp.swapaxes(hidden, 0, 1)
    new_down = trainer_down.astype(jnp.bfloat16)
    return hidden, new_down
```

```python
import functools

import jax
import jax.numpy as jnp
from jax import lax
from jax.experimental import pallas as pl
from jax.experimental.pallas import tpu as pltpu
from jax.sharding import PartitionSpec as P

MESH = pl.DeviceIdType.MESH
CAP = 3
LOADS = 4
WEIGHTS = 3


def pad(x, m):
    return -(-x // m) * m


def owner_at(n, me, dc, dk):
    return lax.rem(me // 2 + dc, n // 2) * 2 + lax.rem(me % 2 + dk, 2)


def kernel(
    n, n_shard, cap, share, share_pad,
    tokens_ref, ids_ref, gate_ref, up_ref, trainer_ref,
    hidden_ref, land_ref,
    rows32, tok_all, ids_all, disp, w_buf, t_buf, send_buf, part, sib, far,
    load_sem, w_sem, own_sem, send_sem, recv_sem,
    tok_send, tok_recv, ids_send, ids_recv, sib_send, sib_recv, far_send, far_recv,
):
    me, me_s = lax.axis_index("owner"), lax.axis_index("shard")
    chips, chip, core = n // 2, me // 2, me % 2
    experts, depth, ff = gate_ref.shape
    rows = trainer_ref.shape[1] // n
    n_rows, top = ids_ref.shape
    pad_rows = tok_all.shape[1]

    far_jobs = [(e, dc, dk) for e in range(experts) for dc in range(1, chips) for dk in (0, 1)]
    near_jobs = [(e, 0, dk) for dk in (1, 0) for e in range(experts)]
    jobs = far_jobs + near_jobs
    early = max(1, len(far_jobs) // 3)

    def load(j):
        e, dc, dk = jobs[j]
        to = owner_at(n, me, dc, dk)
        at = pl.ds(pl.multiple_of(to * rows, rows), rows)
        return pltpu.make_async_copy(
            trainer_ref.at[e, at], t_buf.at[j % LOADS], load_sem.at[j % LOADS]
        )

    def ship(j):
        e, dc, dk = jobs[j]
        if dc == 0 and dk == 0:
            return pltpu.make_async_copy(send_buf.at[j], land_ref.at[e, me], own_sem.at[e])
        return pltpu.make_async_remote_copy(
            src_ref=send_buf.at[j], dst_ref=land_ref.at[e, me],
            send_sem=send_sem.at[j], recv_sem=recv_sem.at[j],
            device_id=(owner_at(n, me, dc, dk), me_s), device_id_type=MESH,
        )

    step = 32 if rows % 32 == 0 else 16

    def run(j):
        load(j).wait()

        def cast(i, _):
            at = pl.ds(pl.multiple_of(i * step, step), step)
            send_buf[j, at] = t_buf[j % LOADS, at].astype(jnp.bfloat16)
            return 0

        lax.fori_loop(0, rows // step, cast, 0)
        if j + LOADS < len(jobs):
            load(j + LOADS).start()
        ship(j).start()

    matrices = [(e, g) for e in range(experts) for g in (0, 1)]

    def weight(i):
        e, g = matrices[i]
        source = (gate_ref, up_ref)[g]
        return pltpu.make_async_copy(source.at[e], w_buf.at[i % WEIGHTS], w_sem.at[i % WEIGHTS])

    for j in range(min(LOADS, len(jobs))):
        load(j).start()

    rows32[...] = jnp.zeros_like(rows32)
    rows32[0:n_rows, :] = tokens_ref[...].astype(jnp.float32)
    tok_all[me_s] = rows32[...].astype(jnp.bfloat16)
    ids_all[me_s] = jnp.full(ids_all.shape[1:], -1, jnp.int32)
    ids_all[me_s, 0:n_rows, 0:top] = ids_ref[...]

    barrier = pltpu.get_barrier_semaphore()
    others = [(dc, dk) for dc in range(chips) for dk in (0, 1) if (dc, dk) != (0, 0)]
    for dc, dk in others:
        pl.semaphore_signal(
            barrier, inc=1, device_id=(owner_at(n, me, dc, dk), me_s), device_id_type=MESH
        )
    for k in range(1, n_shard):
        pl.semaphore_signal(
            barrier, inc=1, device_id=(me, lax.rem(me_s + k, n_shard)), device_id_type=MESH
        )
    pl.semaphore_wait(barrier, n - 1 + n_shard - 1)

    def pass_on(k, ref, sends, recvs):
        return pltpu.make_async_remote_copy(
            src_ref=ref.at[me_s], dst_ref=ref.at[me_s],
            send_sem=sends.at[k], recv_sem=recvs.at[k],
            device_id=(me, lax.rem(me_s + k, n_shard)), device_id_type=MESH,
        )

    token_copies = []
    for k in range(1, n_shard):
        token_copies.append(pass_on(k, tok_all, tok_send, tok_recv))
        token_copies.append(pass_on(k, ids_all, ids_send, ids_recv))
    for copy in token_copies:
        copy.start()

    for j in range(early):
        run(j)
    for i in range(min(WEIGHTS, len(matrices))):
        weight(i).start()
    for copy in token_copies:
        copy.wait()

    all_rows = n_shard * pad_rows
    slots = n * share_pad
    ids = ids_all[...].reshape(all_rows, ids_all.shape[2])
    r = lax.broadcasted_iota(jnp.int32, (all_rows, all_rows), 0)
    q = lax.broadcasted_iota(jnp.int32, (all_rows, all_rows), 1)
    earlier = jnp.where((r // pad_rows == q // pad_rows) & (q < r), 1.0, 0.0).astype(jnp.bfloat16)
    lane = lax.broadcasted_iota(jnp.int32, (all_rows, 128), 1)
    hits = jnp.zeros((all_rows, 128), jnp.float32)
    for k in range(top):
        hits = hits + jnp.where(ids[:, k : k + 1] == me_s * experts + lane, 1.0, 0.0)
    hits = jnp.where(lane < experts, hits, 0.0)
    before = jnp.dot(earlier, hits.astype(jnp.bfloat16), preferred_element_type=jnp.float32)
    before = before.astype(jnp.int32)
    block = lax.broadcasted_iota(jnp.int32, (all_rows, 1), 0) // pad_rows
    place = lax.broadcasted_iota(jnp.int32, (all_rows, slots), 1)
    tokens = tok_all[...].reshape(all_rows, depth)
    for e in range(experts):
        slot = block * cap + before[:, e : e + 1]
        slot = slot // share * share_pad + slot % share
        chosen = jnp.where(place == slot, hits[:, e : e + 1], 0.0).astype(jnp.bfloat16)
        disp[e] = lax.dot_general(
            chosen, tokens, (((0,), (0,)), ((), ())), preferred_element_type=jnp.float32
        ).astype(jnp.bfloat16)

    for i, (e, g) in enumerate(matrices):
        weight(i).wait()
        total = jnp.dot(disp[e], w_buf[i % WEIGHTS], preferred_element_type=jnp.float32)
        for o in range(n):
            part[o, e, g] = total[o * share_pad : (o + 1) * share_pad]
        if i + WEIGHTS < len(matrices):
            weight(i + WEIGHTS).start()

    def to_sibling(c):
        return pltpu.make_async_remote_copy(
            src_ref=part.at[c * 2 + 1 - core], dst_ref=sib.at[c],
            send_sem=sib_send.at[c], recv_sem=sib_recv.at[c],
            device_id=(owner_at(n, me, 0, 1), me_s), device_id_type=MESH,
        )

    def to_chip(dc):
        c = lax.rem(chip + dc, chips)
        return pltpu.make_async_remote_copy(
            src_ref=part.at[c * 2 + core], dst_ref=far.at[dc],
            send_sem=far_send.at[dc], recv_sem=far_recv.at[dc],
            device_id=(owner_at(n, me, dc, 0), me_s), device_id_type=MESH,
        )

    for c in range(chips):
        to_sibling(c).start()
    for c in range(chips):
        to_sibling(c).wait()
    for c in range(chips):
        part[c * 2 + core] = part[c * 2 + core] + sib[c]
    for dc in range(1, chips):
        to_chip(dc).start()

    for j in range(early, len(jobs)):
        run(j)

    for dc in range(1, chips):
        to_chip(dc).wait()
    for e in range(experts):
        gate, up = part[me, e, 0], part[me, e, 1]
        for dc in range(1, chips):
            gate, up = gate + far[dc, e, 0], up + far[dc, e, 1]
        hidden_ref[e] = gate / (1.0 + jnp.exp(-gate)) * up

    for j in range(len(jobs)):
        ship(j).wait()


def exchange(tokens, expert_ids, gate_weight, up_weight, trainer_down):
    n, n_shard = lax.axis_size("owner"), lax.axis_size("shard")
    experts, depth, ff = gate_weight.shape
    width, rows = trainer_down.shape[2], trainer_down.shape[1] // n
    n_rows, top = expert_ids.shape
    share = CAP * n_shard // n
    share_pad = pad(share, 8)
    pad_rows = pad(n_rows, 16)
    count = experts * n
    dma = pltpu.SemaphoreType.DMA
    whole = pl.BlockSpec(memory_space=pltpu.VMEM)
    remote = pl.BlockSpec(memory_space=pl.ANY)
    return pl.pallas_call(
        functools.partial(kernel, n, n_shard, CAP, share, share_pad),
        out_shape=(
            jax.ShapeDtypeStruct((experts, share_pad, ff), jnp.float32),
            jax.ShapeDtypeStruct((experts, n, rows, width), jnp.bfloat16),
        ),
        in_specs=[whole, whole, remote, remote, remote],
        out_specs=(whole, remote),
        scratch_shapes=[
            pltpu.VMEM((pad_rows, depth), jnp.float32),
            pltpu.VMEM((n_shard, pad_rows, depth), jnp.bfloat16),
            pltpu.VMEM((n_shard, pad_rows, 128), jnp.int32),
            pltpu.VMEM((experts, n * share_pad, depth), jnp.bfloat16),
            pltpu.VMEM((WEIGHTS, depth, ff), jnp.bfloat16),
            pltpu.VMEM((LOADS, rows, width), jnp.float32),
            pltpu.VMEM((count, rows, width), jnp.bfloat16),
            pltpu.VMEM((n, experts, 2, share_pad, ff), jnp.float32),
            pltpu.VMEM((n // 2, experts, 2, share_pad, ff), jnp.float32),
            pltpu.VMEM((n // 2, experts, 2, share_pad, ff), jnp.float32),
            dma((LOADS,)), dma((WEIGHTS,)), dma((experts,)), dma((count,)), dma((count,)),
            dma((n_shard,)), dma((n_shard,)), dma((n_shard,)), dma((n_shard,)),
            dma((n // 2,)), dma((n // 2,)), dma((n // 2,)), dma((n // 2,)),
        ],
        compiler_params=pltpu.CompilerParams(
            collective_id=0, has_side_effects=True, vmem_limit_bytes=56 * 2**20
        ),
        cost_estimate=pl.CostEstimate(
            flops=4 * experts * n * share_pad * depth * ff,
            bytes_accessed=4 * experts * depth * ff + 6 * experts * n * rows * width,
            transcendentals=experts * share_pad * ff,
        ),
        name="exchange",
    )(tokens, expert_ids, gate_weight, up_weight, trainer_down)


def place_body(x_ref, o_ref):
    o_ref[0] = x_ref[0, 0]


def lay_out(landed):
    experts, n, rows, width = landed.shape
    if width % 128:
        return landed.transpose(0, 2, 1, 3).reshape(experts, rows, n * width)
    return pl.pallas_call(
        place_body,
        grid=(experts, n),
        in_specs=[pl.BlockSpec((1, 1, rows, width), lambda e, o: (e, o, 0, 0))],
        out_specs=pl.BlockSpec((1, rows, width), lambda e, o: (e, 0, o)),
        out_shape=jax.ShapeDtypeStruct((experts, rows, n * width), landed.dtype),
        compiler_params=pltpu.CompilerParams(vmem_limit_bytes=56 * 2**20),
        cost_estimate=pl.CostEstimate(
            flops=0, bytes_accessed=4 * landed.size, transcendentals=0
        ),
        name="lay_out",
    )(landed)


def on_device(tokens, expert_ids, gate_weight, up_weight, trainer_down):
    share = CAP * lax.axis_size("shard") // lax.axis_size("owner")
    hidden, landed = exchange(tokens, expert_ids, gate_weight, up_weight, trainer_down)
    hidden = jnp.swapaxes(hidden[:, :share], 0, 1).astype(jnp.bfloat16)
    return (hidden, lay_out(landed))


def solution(mesh):
    in_specs = (
        P("shard", "owner"),
        P("shard", None),
        P("shard", "owner", None),
        P("shard", "owner", None),
        P("shard", None, "owner"),
    )
    out_specs = (P("owner", "shard", None), P("shard", "owner", None))
    return jax.shard_map(
        on_device, mesh=mesh, in_specs=in_specs, out_specs=out_specs, check_vma=False
    )
```

```python
import functools

import jax
import jax.numpy as jnp
from jax import lax
from jax.experimental import pallas as pl
from jax.experimental.pallas import tpu as pltpu
from jax.sharding import PartitionSpec as P

MESH = pl.DeviceIdType.MESH
CAP = 3
LOADS = 4
WEIGHTS = 3


def pad(x, m):
    return -(-x // m) * m


def owner_at(n, me, dc, dk):
    return lax.rem(me // 2 + dc, n // 2) * 2 + lax.rem(me % 2 + dk, 2)


def kernel(
    n, n_shard, cap, share, share_pad,
    tokens_ref, ids_ref, gate_ref, up_ref, trainer_ref,
    hidden_ref, land_ref,
    rows32, tok_all, ids_all, disp, w_buf, t_buf, send_buf, part, sib, far,
    load_sem, w_sem, own_sem, send_sem, recv_sem,
    tok_send, tok_recv, ids_send, ids_recv, sib_send, sib_recv, far_send, far_recv,
):
    me, me_s = lax.axis_index("owner"), lax.axis_index("shard")
    chips, chip, core = n // 2, me // 2, me % 2
    experts, depth, ff = gate_ref.shape
    rows = trainer_ref.shape[1] // n
    top, n_rows = ids_ref.shape
    pairs = share * 2
    pad_rows = tok_all.shape[1]

    far_jobs = [(e, dc, dk) for e in range(experts) for dc in range(1, chips) for dk in (0, 1)]
    near_jobs = [(e, 0, dk) for dk in (1, 0) for e in range(experts)]
    jobs = far_jobs + near_jobs
    early = max(1, len(far_jobs) // 3)

    def load(j):
        e, dc, dk = jobs[j]
        to = owner_at(n, me, dc, dk)
        at = pl.ds(pl.multiple_of(to * rows, rows), rows)
        return pltpu.make_async_copy(
            trainer_ref.at[e, at], t_buf.at[j % LOADS], load_sem.at[j % LOADS]
        )

    def ship(j):
        e, dc, dk = jobs[j]
        if dc == 0 and dk == 0:
            return pltpu.make_async_copy(send_buf.at[j], land_ref.at[e, me], own_sem.at[e])
        return pltpu.make_async_remote_copy(
            src_ref=send_buf.at[j], dst_ref=land_ref.at[e, me],
            send_sem=send_sem.at[j], recv_sem=recv_sem.at[j],
            device_id=(owner_at(n, me, dc, dk), me_s), device_id_type=MESH,
        )

    step = 32 if rows % 32 == 0 else 16

    def run(j):
        load(j).wait()

        def cast(i, _):
            at = pl.ds(pl.multiple_of(i * step, step), step)
            send_buf[j, at] = t_buf[j % LOADS, at].astype(jnp.bfloat16)
            return 0

        lax.fori_loop(0, rows // step, cast, 0)
        if j + LOADS < len(jobs):
            load(j + LOADS).start()
        ship(j).start()

    matrices = [(e, g) for e in range(experts) for g in (0, 1)]

    def weight(i):
        e, g = matrices[i]
        source = (gate_ref, up_ref)[g]
        return pltpu.make_async_copy(source.at[e], w_buf.at[i % WEIGHTS], w_sem.at[i % WEIGHTS])

    for j in range(min(LOADS, len(jobs))):
        load(j).start()

    rows32[...] = jnp.zeros_like(rows32)
    rows32[0:n_rows, :] = tokens_ref[...].astype(jnp.float32)
    tok_all[me_s] = rows32[...].astype(jnp.bfloat16)
    ids_all[me_s] = jnp.full(ids_all.shape[1:], -1, jnp.int32)
    ids_all[me_s, 0:n_rows, 0:top] = ids_ref[...].T

    barrier = pltpu.get_barrier_semaphore()
    others = [(dc, dk) for dc in range(chips) for dk in (0, 1) if (dc, dk) != (0, 0)]
    for dc, dk in others:
        pl.semaphore_signal(
            barrier, inc=1, device_id=(owner_at(n, me, dc, dk), me_s), device_id_type=MESH
        )
    for k in range(1, n_shard):
        pl.semaphore_signal(
            barrier, inc=1, device_id=(me, lax.rem(me_s + k, n_shard)), device_id_type=MESH
        )
    pl.semaphore_wait(barrier, n - 1 + n_shard - 1)

    def pass_on(k, ref, sends, recvs):
        return pltpu.make_async_remote_copy(
            src_ref=ref.at[me_s], dst_ref=ref.at[me_s],
            send_sem=sends.at[k], recv_sem=recvs.at[k],
            device_id=(me, lax.rem(me_s + k, n_shard)), device_id_type=MESH,
        )

    token_copies = []
    for k in range(1, n_shard):
        token_copies.append(pass_on(k, tok_all, tok_send, tok_recv))
        token_copies.append(pass_on(k, ids_all, ids_send, ids_recv))
    run(0)
    for copy in token_copies:
        copy.start()

    for j in range(1, early):
        run(j)
    for i in range(min(WEIGHTS, len(matrices))):
        weight(i).start()
    for copy in token_copies:
        copy.wait()

    all_rows = n_shard * pad_rows
    slots = n * share_pad
    ids = ids_all[...].reshape(all_rows, ids_all.shape[2])
    r = lax.broadcasted_iota(jnp.int32, (all_rows, all_rows), 0)
    q = lax.broadcasted_iota(jnp.int32, (all_rows, all_rows), 1)
    earlier = jnp.where((r // pad_rows == q // pad_rows) & (q < r), 1.0, 0.0).astype(jnp.bfloat16)
    lane = lax.broadcasted_iota(jnp.int32, (all_rows, 128), 1)
    hits = jnp.zeros((all_rows, 128), jnp.float32)
    for k in range(top):
        hits = hits + jnp.where(ids[:, k : k + 1] == me_s * experts + lane, 1.0, 0.0)
    hits = jnp.where(lane < experts, hits, 0.0)
    before = jnp.dot(earlier, hits.astype(jnp.bfloat16), preferred_element_type=jnp.float32)
    before = before.astype(jnp.int32)
    block = lax.broadcasted_iota(jnp.int32, (all_rows, 1), 0) // pad_rows
    place = lax.broadcasted_iota(jnp.int32, (all_rows, slots), 1)
    tokens = tok_all[...].reshape(all_rows, depth)
    for e in range(experts):
        slot = block * cap + before[:, e : e + 1]
        slot = slot // share * share_pad + slot % share
        chosen = jnp.where(place == slot, hits[:, e : e + 1], 0.0).astype(jnp.bfloat16)
        disp[e] = lax.dot_general(
            chosen, tokens, (((0,), (0,)), ((), ())), preferred_element_type=jnp.float32
        ).astype(jnp.bfloat16)

    for i, (e, g) in enumerate(matrices):
        weight(i).wait()
        total = jnp.dot(disp[e], w_buf[i % WEIGHTS], preferred_element_type=jnp.float32)
        for o in range(n):
            at = e * pairs + g * share
            part[o, at : at + share] = total[o * share_pad : o * share_pad + share]
        if i + WEIGHTS < len(matrices):
            weight(i + WEIGHTS).start()

    def to_sibling(c):
        return pltpu.make_async_remote_copy(
            src_ref=part.at[c * 2 + 1 - core], dst_ref=sib.at[c],
            send_sem=sib_send.at[c], recv_sem=sib_recv.at[c],
            device_id=(owner_at(n, me, 0, 1), me_s), device_id_type=MESH,
        )

    def to_chip(dc):
        c = lax.rem(chip + dc, chips)
        return pltpu.make_async_remote_copy(
            src_ref=part.at[c * 2 + core], dst_ref=far.at[dc],
            send_sem=far_send.at[dc], recv_sem=far_recv.at[dc],
            device_id=(owner_at(n, me, dc, 0), me_s), device_id_type=MESH,
        )

    for c in range(chips):
        to_sibling(c).start()
    for c in range(chips):
        to_sibling(c).wait()
    for c in range(chips):
        part[c * 2 + core] = part[c * 2 + core] + sib[c]
    for dc in range(1, chips):
        to_chip(dc).start()

    for j in range(early, len(jobs)):
        run(j)

    for dc in range(1, chips):
        to_chip(dc).wait()
    for e in range(experts):
        at = e * pairs
        both = part[me, at : at + pairs]
        for dc in range(1, chips):
            both = both + far[dc, at : at + pairs]
        gate, up = both[:share], both[share:]
        value = gate / (1.0 + jnp.exp(-gate)) * up
        for s in range(share):
            hidden_ref[s, e : e + 1] = value[s : s + 1]

    for j in range(len(jobs)):
        ship(j).wait()


def exchange(tokens, expert_ids, gate_weight, up_weight, trainer_down):
    n, n_shard = lax.axis_size("owner"), lax.axis_size("shard")
    experts, depth, ff = gate_weight.shape
    width, rows = trainer_down.shape[2], trainer_down.shape[1] // n
    n_rows, top = expert_ids.shape
    share = CAP * n_shard // n
    share_pad = pad(share, 8)
    pad_rows = pad(n_rows, 16)
    count = experts * n
    sums = pad(experts * 2 * share, 8)
    dma = pltpu.SemaphoreType.DMA
    whole = pl.BlockSpec(memory_space=pltpu.VMEM)
    remote = pl.BlockSpec(memory_space=pl.ANY)
    return pl.pallas_call(
        functools.partial(kernel, n, n_shard, CAP, share, share_pad),
        out_shape=(
            jax.ShapeDtypeStruct((share, experts, ff), jnp.float32),
            jax.ShapeDtypeStruct((experts, n, rows, width), jnp.bfloat16),
        ),
        in_specs=[whole, whole, remote, remote, remote],
        out_specs=(whole, remote),
        scratch_shapes=[
            pltpu.VMEM((pad_rows, depth), jnp.float32),
            pltpu.VMEM((n_shard, pad_rows, depth), jnp.bfloat16),
            pltpu.VMEM((n_shard, pad_rows, 128), jnp.int32),
            pltpu.VMEM((experts, n * share_pad, depth), jnp.bfloat16),
            pltpu.VMEM((WEIGHTS, depth, ff), jnp.bfloat16),
            pltpu.VMEM((LOADS, rows, width), jnp.float32),
            pltpu.VMEM((count, rows, width), jnp.bfloat16),
            pltpu.VMEM((n, sums, ff), jnp.float32),
            pltpu.VMEM((n // 2, sums, ff), jnp.float32),
            pltpu.VMEM((n // 2, sums, ff), jnp.float32),
            dma((LOADS,)), dma((WEIGHTS,)), dma((experts,)), dma((count,)), dma((count,)),
            dma((n_shard,)), dma((n_shard,)), dma((n_shard,)), dma((n_shard,)),
            dma((n // 2,)), dma((n // 2,)), dma((n // 2,)), dma((n // 2,)),
        ],
        compiler_params=pltpu.CompilerParams(
            collective_id=0, has_side_effects=True, vmem_limit_bytes=56 * 2**20
        ),
        cost_estimate=pl.CostEstimate(
            flops=4 * experts * n * share_pad * depth * ff,
            bytes_accessed=4 * experts * depth * ff + 6 * experts * n * rows * width,
            transcendentals=experts * share_pad * ff,
        ),
        name="exchange",
    )(tokens, expert_ids.T, gate_weight, up_weight, trainer_down)


def place_body(landed_ref, value_ref, out_ref, hidden_ref, buf, in_sem, out_sem):
    experts, n, rows, width = landed_ref.shape
    blocks = [(e, o) for e in range(experts) for o in range(n)]

    def fetch(e, o):
        return pltpu.make_async_copy(landed_ref.at[e, o], buf.at[e, o], in_sem.at[e, o])

    def store(e, o):
        to = out_ref.at[e, :, pl.ds(o * width, width)]
        return pltpu.make_async_copy(buf.at[e, o], to, out_sem.at[e, o])

    for e, o in blocks:
        fetch(e, o).start()
    hidden_ref[...] = value_ref[...].astype(hidden_ref.dtype)
    for e, o in blocks:
        fetch(e, o).wait()
        store(e, o).start()
    for e, o in blocks:
        store(e, o).wait()


def lay_out(landed, value):
    experts, n, rows, width = landed.shape
    if width % 128:
        landed = landed.transpose(0, 2, 1, 3).reshape(experts, rows, n * width)
        return value.astype(landed.dtype), landed
    whole = pl.BlockSpec(memory_space=pltpu.VMEM)
    remote = pl.BlockSpec(memory_space=pl.ANY)
    out, hidden = pl.pallas_call(
        place_body,
        in_specs=[remote, whole],
        out_specs=(remote, whole),
        out_shape=(
            jax.ShapeDtypeStruct((experts, rows, n * width), landed.dtype),
            jax.ShapeDtypeStruct(value.shape, landed.dtype),
        ),
        scratch_shapes=[
            pltpu.VMEM(landed.shape, landed.dtype),
            pltpu.SemaphoreType.DMA((experts, n)), pltpu.SemaphoreType.DMA((experts, n)),
        ],
        compiler_params=pltpu.CompilerParams(vmem_limit_bytes=56 * 2**20),
        cost_estimate=pl.CostEstimate(
            flops=0, bytes_accessed=4 * landed.size, transcendentals=0
        ),
        name="lay_out",
    )(landed, value)
    return hidden, out


def on_device(tokens, expert_ids, gate_weight, up_weight, trainer_down):
    value, landed = exchange(tokens, expert_ids, gate_weight, up_weight, trainer_down)
    return lay_out(landed, value)


def solution(mesh):
    in_specs = (
        P("shard", "owner"),
        P("shard", None),
        P("shard", "owner", None),
        P("shard", "owner", None),
        P("shard", None, "owner"),
    )
    out_specs = (P("owner", "shard", None), P("shard", "owner", None))
    return jax.shard_map(
        on_device, mesh=mesh, in_specs=in_specs, out_specs=out_specs, check_vma=False
    )
```

```python
import functools

import jax
import jax.numpy as jnp
from jax import lax
from jax.experimental import pallas as pl
from jax.experimental.pallas import tpu as pltpu
from jax.sharding import PartitionSpec as P

MESH = pl.DeviceIdType.MESH
CAP = 3
LOADS = 4
WEIGHTS = 2


def pad(x, m):
    return -(-x // m) * m


def owner_at(n, me, dc, dk):
    return lax.rem(me // 2 + dc, n // 2) * 2 + lax.rem(me % 2 + dk, 2)


def kernel(
    n, n_shard, cap, share, share_pad,
    tokens_ref, ids_ref, gate_ref, up_ref, trainer_ref,
    hidden_ref, land_ref,
    rows32, tok_all, ids_all, disp, w_buf, t_buf, send_buf, part, sib, far,
    load_sem, w_sem, send_sem, recv_sem,
    tok_send, tok_recv, ids_send, ids_recv, sib_send, sib_recv, far_send, far_recv,
):
    me, me_s = lax.axis_index("owner"), lax.axis_index("shard")
    chips, chip, core = n // 2, me // 2, me % 2
    experts, depth, ff = gate_ref.shape
    rows = trainer_ref.shape[1] // n
    top, n_rows = ids_ref.shape
    pairs = share * 2
    pad_rows = tok_all.shape[1]

    far_jobs = [(e, dc, dk) for e in range(experts) for dc in range(1, chips) for dk in (0, 1)]
    near_jobs = [(e, 0, dk) for dk in (1, 0) for e in range(experts)]
    jobs = far_jobs + near_jobs
    early = max(1, len(far_jobs) // 3)

    def load(j):
        e, dc, dk = jobs[j]
        to = owner_at(n, me, dc, dk)
        at = pl.ds(pl.multiple_of(to * rows, rows), rows)
        return pltpu.make_async_copy(
            trainer_ref.at[e, at], t_buf.at[j % LOADS], load_sem.at[j % LOADS]
        )

    def ship(j):
        e, dc, dk = jobs[j]
        return pltpu.make_async_remote_copy(
            src_ref=send_buf.at[j], dst_ref=land_ref.at[e, me],
            send_sem=send_sem.at[j], recv_sem=recv_sem.at[j],
            device_id=(owner_at(n, me, dc, dk), me_s), device_id_type=MESH,
        )

    step = 32 if rows % 32 == 0 else 16

    def run(j):
        load(j).wait()
        e, dc, dk = jobs[j]
        own = dc == 0 and dk == 0

        def cast(i, _):
            at = pl.ds(pl.multiple_of(i * step, step), step)
            block = t_buf[j % LOADS, at].astype(jnp.bfloat16)
            if own:
                land_ref[e, me, at] = block
            else:
                send_buf[j, at] = block
            return 0

        lax.fori_loop(0, rows // step, cast, 0)
        if j + LOADS < len(jobs):
            load(j + LOADS).start()
        if not own:
            ship(j).start()

    matrices = [(e, g) for e in range(experts) for g in (0, 1)]

    def weight(i):
        e, g = matrices[i]
        source = (gate_ref, up_ref)[g]
        return pltpu.make_async_copy(source.at[e], w_buf.at[i % WEIGHTS], w_sem.at[i % WEIGHTS])

    for j in range(min(LOADS, len(jobs))):
        load(j).start()

    rows32[...] = jnp.zeros_like(rows32)
    rows32[0:n_rows, :] = tokens_ref[...].astype(jnp.float32)
    tok_all[me_s] = rows32[...].astype(jnp.bfloat16)
    ids_all[me_s] = jnp.full(ids_all.shape[1:], -1, jnp.int32)
    ids_all[me_s, 0:n_rows, 0:top] = ids_ref[...].T

    barrier = pltpu.get_barrier_semaphore()
    others = [(dc, dk) for dc in range(chips) for dk in (0, 1) if (dc, dk) != (0, 0)]
    for dc, dk in others:
        pl.semaphore_signal(
            barrier, inc=1, device_id=(owner_at(n, me, dc, dk), me_s), device_id_type=MESH
        )
    for k in range(1, n_shard):
        pl.semaphore_signal(
            barrier, inc=1, device_id=(me, lax.rem(me_s + k, n_shard)), device_id_type=MESH
        )
    pl.semaphore_wait(barrier, n - 1 + n_shard - 1)

    def pass_on(k, ref, sends, recvs):
        return pltpu.make_async_remote_copy(
            src_ref=ref.at[me_s], dst_ref=ref.at[me_s],
            send_sem=sends.at[k], recv_sem=recvs.at[k],
            device_id=(me, lax.rem(me_s + k, n_shard)), device_id_type=MESH,
        )

    token_copies = []
    for k in range(1, n_shard):
        token_copies.append(pass_on(k, tok_all, tok_send, tok_recv))
        token_copies.append(pass_on(k, ids_all, ids_send, ids_recv))
    run(0)
    for copy in token_copies:
        copy.start()

    for j in range(1, early):
        run(j)
    for i in range(min(WEIGHTS, len(matrices))):
        weight(i).start()
    for copy in token_copies:
        copy.wait()

    all_rows = n_shard * pad_rows
    slots = n * share_pad
    ids = ids_all[...].reshape(all_rows, ids_all.shape[2])
    r = lax.broadcasted_iota(jnp.int32, (all_rows, all_rows), 0)
    q = lax.broadcasted_iota(jnp.int32, (all_rows, all_rows), 1)
    earlier = jnp.where((r // pad_rows == q // pad_rows) & (q < r), 1.0, 0.0).astype(jnp.bfloat16)
    lane = lax.broadcasted_iota(jnp.int32, (all_rows, 128), 1)
    hits = jnp.zeros((all_rows, 128), jnp.float32)
    for k in range(top):
        hits = hits + jnp.where(ids[:, k : k + 1] == me_s * experts + lane, 1.0, 0.0)
    hits = jnp.where(lane < experts, hits, 0.0)
    before = jnp.dot(earlier, hits.astype(jnp.bfloat16), preferred_element_type=jnp.float32)
    before = before.astype(jnp.int32)
    block = lax.broadcasted_iota(jnp.int32, (all_rows, 1), 0) // pad_rows
    place = lax.broadcasted_iota(jnp.int32, (all_rows, slots), 1)
    tokens = tok_all[...].reshape(all_rows, depth)
    for e in range(experts):
        slot = block * cap + before[:, e : e + 1]
        slot = slot // share * share_pad + slot % share
        chosen = jnp.where(place == slot, hits[:, e : e + 1], 0.0).astype(jnp.bfloat16)
        disp[e] = lax.dot_general(
            chosen, tokens, (((0,), (0,)), ((), ())), preferred_element_type=jnp.float32
        ).astype(jnp.bfloat16)

    for i, (e, g) in enumerate(matrices):
        weight(i).wait()
        total = jnp.dot(disp[e], w_buf[i % WEIGHTS], preferred_element_type=jnp.float32)
        for o in range(n):
            at = e * pairs + g * share
            part[o, at : at + share] = total[o * share_pad : o * share_pad + share]
        if i + WEIGHTS < len(matrices):
            weight(i + WEIGHTS).start()

    def to_sibling(c):
        return pltpu.make_async_remote_copy(
            src_ref=part.at[c * 2 + 1 - core], dst_ref=sib.at[c],
            send_sem=sib_send.at[c], recv_sem=sib_recv.at[c],
            device_id=(owner_at(n, me, 0, 1), me_s), device_id_type=MESH,
        )

    def to_chip(dc):
        c = lax.rem(chip + dc, chips)
        return pltpu.make_async_remote_copy(
            src_ref=part.at[c * 2 + core], dst_ref=far.at[dc],
            send_sem=far_send.at[dc], recv_sem=far_recv.at[dc],
            device_id=(owner_at(n, me, dc, 0), me_s), device_id_type=MESH,
        )

    for c in range(chips):
        to_sibling(c).start()
    for c in range(chips):
        to_sibling(c).wait()
    for c in range(chips):
        part[c * 2 + core] = part[c * 2 + core] + sib[c]
    for dc in range(1, chips):
        to_chip(dc).start()

    for j in range(early, len(jobs)):
        run(j)

    for dc in range(1, chips):
        to_chip(dc).wait()
    for e in range(experts):
        at = e * pairs
        both = part[me, at : at + pairs]
        for dc in range(1, chips):
            both = both + far[dc, at : at + pairs]
        gate, up = both[:share], both[share:]
        value = gate / (1.0 + jnp.exp(-gate)) * up
        for s in range(share):
            hidden_ref[s, e : e + 1] = value[s : s + 1]

    for j in range(len(jobs) - experts):
        ship(j).wait()


def exchange(tokens, expert_ids, gate_weight, up_weight, trainer_down):
    n, n_shard = lax.axis_size("owner"), lax.axis_size("shard")
    experts, depth, ff = gate_weight.shape
    width, rows = trainer_down.shape[2], trainer_down.shape[1] // n
    n_rows, top = expert_ids.shape
    share = CAP * n_shard // n
    share_pad = pad(share, 8)
    pad_rows = pad(n_rows, 16)
    count = experts * (n - 1)
    sums = pad(experts * 2 * share, 8)
    dma = pltpu.SemaphoreType.DMA
    whole = pl.BlockSpec(memory_space=pltpu.VMEM)
    remote = pl.BlockSpec(memory_space=pl.ANY)
    return pl.pallas_call(
        functools.partial(kernel, n, n_shard, CAP, share, share_pad),
        out_shape=(
            pltpu.VMEM((share, experts, ff), jnp.float32),
            pltpu.VMEM((experts, n, rows, width), jnp.bfloat16),
        ),
        in_specs=[whole, whole, remote, remote, remote],
        out_specs=(whole, whole),
        scratch_shapes=[
            pltpu.VMEM((pad_rows, depth), jnp.float32),
            pltpu.VMEM((n_shard, pad_rows, depth), jnp.bfloat16),
            pltpu.VMEM((n_shard, pad_rows, 128), jnp.int32),
            pltpu.VMEM((experts, n * share_pad, depth), jnp.bfloat16),
            pltpu.VMEM((WEIGHTS, depth, ff), jnp.bfloat16),
            pltpu.VMEM((LOADS, rows, width), jnp.float32),
            pltpu.VMEM((count, rows, width), jnp.bfloat16),
            pltpu.VMEM((n, sums, ff), jnp.float32),
            pltpu.VMEM((n // 2, sums, ff), jnp.float32),
            pltpu.VMEM((n // 2, sums, ff), jnp.float32),
            dma((LOADS,)), dma((WEIGHTS,)), dma((count,)), dma((count,)),
            dma((n_shard,)), dma((n_shard,)), dma((n_shard,)), dma((n_shard,)),
            dma((n // 2,)), dma((n // 2,)), dma((n // 2,)), dma((n // 2,)),
        ],
        compiler_params=pltpu.CompilerParams(
            collective_id=0, has_side_effects=True, vmem_limit_bytes=38 * 2**20
        ),
        cost_estimate=pl.CostEstimate(
            flops=4 * experts * n * share_pad * depth * ff,
            bytes_accessed=4 * experts * depth * ff + 4 * experts * n * rows * width,
            transcendentals=experts * share_pad * ff,
        ),
        name="exchange",
    )(tokens, expert_ids.T, gate_weight, up_weight, trainer_down)


def place_body(landed_ref, value_ref, out_ref, hidden_ref, out_sem):
    experts, n, rows, width = landed_ref.shape
    blocks = [(e, o) for e in range(experts) for o in range(n)]

    def store(e, o):
        to = out_ref.at[e, :, pl.ds(o * width, width)]
        return pltpu.make_async_copy(landed_ref.at[e, o], to, out_sem.at[e, o])

    for e, o in blocks:
        store(e, o).start()
    hidden_ref[...] = value_ref[...].astype(hidden_ref.dtype)
    for e, o in blocks:
        store(e, o).wait()


def lay_out(landed, value):
    experts, n, rows, width = landed.shape
    if width % 128:
        landed = landed.transpose(0, 2, 1, 3).reshape(experts, rows, n * width)
        return value.astype(landed.dtype), landed
    whole = pl.BlockSpec(memory_space=pltpu.VMEM)
    remote = pl.BlockSpec(memory_space=pl.ANY)
    out, hidden = pl.pallas_call(
        place_body,
        in_specs=[whole, whole],
        out_specs=(remote, whole),
        out_shape=(
            jax.ShapeDtypeStruct((experts, rows, n * width), landed.dtype),
            jax.ShapeDtypeStruct(value.shape, landed.dtype),
        ),
        scratch_shapes=[pltpu.SemaphoreType.DMA((experts, n))],
        compiler_params=pltpu.CompilerParams(vmem_limit_bytes=32 * 2**20),
        cost_estimate=pl.CostEstimate(
            flops=0, bytes_accessed=2 * landed.size, transcendentals=0
        ),
        name="lay_out",
    )(landed, value)
    return hidden, out


def on_device(tokens, expert_ids, gate_weight, up_weight, trainer_down):
    value, landed = exchange(tokens, expert_ids, gate_weight, up_weight, trainer_down)
    return lay_out(landed, value)


def solution(mesh):
    in_specs = (
        P("shard", "owner"),
        P("shard", None),
        P("shard", "owner", None),
        P("shard", "owner", None),
        P("shard", None, "owner"),
    )
    out_specs = (P("owner", "shard", None), P("shard", "owner", None))
    return jax.shard_map(
        on_device, mesh=mesh, in_specs=in_specs, out_specs=out_specs, check_vma=False
    )
```
